256 devices in a mesh: res: 128 (over x, z, y_lo, core), ch: 2 (over y_hi).
Axes of the slice: x: 4, y: 4 (y_hi: 2, y_lo: 2; y = y_hi * 2 + y_lo), z: 8, core: 2. Of those that a mesh axis runs over, the one named last changes fastest.
Arguments:
- pair: bfloat16 [512, 512, 128], P('res'), may hold values from -48 to 48
- norm_gain: float32 [128], replicated, may hold values from 0.4 to 1.6
- norm_bias: float32 [128], replicated, may hold values from -2.5 to 2.5
- left_weight: bfloat16 [128, 128], P(None, 'ch'), may hold values from -0.5 to 0.5
- left_gate: bfloat16 [128, 128], P(None, 'ch'), may hold values from -0.5 to 0.5
- right_weight: bfloat16 [128, 128], P(None, 'ch'), may hold values from -0.5 to 0.5
- right_gate: bfloat16 [128, 128], P(None, 'ch'), may hold values from -0.5 to 0.5
- tri_gain: float32 [128], P('ch'), may hold values from 0.4 to 1.6
- tri_bias: float32 [128], P('ch'), may hold values from -2.5 to 2.5
- out_weight: bfloat16 [128, 128], P('ch'), may hold values from -0.5 to 0.5
- out_gate: bfloat16 [128, 128], P(None, 'ch'), may hold values from -0.5 to 0.5
Outputs:
- updated: bfloat16 [512, 512, 128], P('res', None, 'ch')
The draws below stay inside these ranges and needn't reach their ends.
All inputs are finite; a program needn't handle non-finite values.
Results may differ from the reference program's by a relative error of at most 0.0055.
Values may be sent and summed in bfloat16 or wider, within the bound.
No kernel may reach another device: no remote copies, remote signals or barrier semaphores. Data moves between devices by JAX's collectives and lax.ppermute only.
A program may use at most 192 MiB of HBM per device.

```python
import math
import jax
import jax.numpy as jnp
from jax import lax

C = 128
N = 512


def draw_pair(key, part):
    key = jax.random.fold_in(key, 11)
    key_chan, key_cell, key_base = jax.random.split(key, 3)
    channel_scale = jnp.exp(jax.random.uniform(key_chan, (C,), jnp.float32, 0.0, math.log(10.0)))
    cell_scale = jnp.exp(jax.random.uniform(key_cell, (N, N, 1), jnp.float32, 0.0, math.log(4.0)))
    base = jnp.clip(jax.random.normal(key_base, (N, N, C), jnp.float32), -4.0, 4.0)
    return (base * channel_scale * cell_scale * 0.3).astype(jnp.bfloat16)


def steps_of(own_key, dims, cuts, least, top_value):
    loudness = 1.0
    for axis_at, blocks in cuts:
        heights = jax.random.uniform(jax.random.fold_in(jax.random.fold_in(own_key, 6), axis_at), (blocks,), jnp.float32, least / len(cuts), top_value / len(cuts))
        loudness = loudness * jnp.repeat(jnp.exp(heights), dims[axis_at] // blocks).reshape((-1,) + (1,) * (len(dims) - 1 - axis_at))
    return loudness


def noise(stream_key, extent, deviation, reach, shards=(), kind=jnp.bfloat16):
    drawn = jax.random.normal(stream_key, extent, jnp.float32) * deviation
    if len(shards) > 0:
        drawn = steps_of(stream_key, extent, shards, -0.22, 0.18) * drawn
    return jnp.clip(drawn, min=-reach, max=reach).astype(kind)


def setup_inputs(seed: int = 0) -> dict:
    splits = jax.random.split(jax.random.key(seed), 12)
    return {
        "pair": draw_pair(jax.random.fold_in(splits[11], 71), 0),
        "norm_gain": jnp.clip(1.0 + 0.12 * jax.random.normal(splits[1], (C,), jnp.float32), 0.4, 1.6),
        "norm_bias": noise(splits[2], (C,), 0.5, 2.5, (), jnp.float32),
        "left_weight": noise(splits[3], (C, C), C ** -0.5, 0.5, ((1, 2),)),
        "left_gate": noise(splits[4], (C, C), C ** -0.5, 0.5, ((1, 2),)),
        "right_weight": noise(splits[5], (C, C), C ** -0.5, 0.5, ((1, 2),)),
        "right_gate": noise(splits[6], (C, C), C ** -0.5, 0.5, ((1, 2),)),
        "tri_gain": jnp.clip(1.0 + 0.12 * jax.random.normal(splits[7], (C,), jnp.float32), 0.4, 1.6),
        "tri_bias": noise(splits[8], (C,), 0.5, 2.5, ((0, 2),), jnp.float32),
        "out_weight": noise(splits[9], (C, C), C ** -0.5, 0.5, ((0, 2),)),
        "out_gate": noise(splits[10], (C, C), C ** -0.5, 0.5, ((1, 2),)),
    }


def layer_norm(values, gain, bias):
    values = values.astype(jnp.float32)
    row_mean = lax.optimization_barrier(jnp.mean(values, -1, keepdims=True))
    centred = values - row_mean
    row_var = lax.optimization_barrier(jnp.mean(centred * centred, -1, keepdims=True))
    return centred * lax.rsqrt(row_var + 1e-05) * gain + bias

def matmul(values, weight):
    flat = values.reshape(-1, values.shape[-1])
    result = jnp.dot(flat, weight, preferred_element_type=jnp.float32)
    return result.reshape(values.shape[:-1] + (weight.shape[1],))

def reference(pair, norm_gain, norm_bias, left_weight, left_gate, right_weight, right_gate, tri_gain, tri_bias, out_weight, out_gate):
    normed = layer_norm(pair, norm_gain, norm_bias).astype(jnp.bfloat16)
    left_proj = (jax.nn.sigmoid(matmul(normed, left_gate)) * matmul(normed, left_weight)).astype(jnp.bfloat16)
    right_proj = (jax.nn.sigmoid(matmul(normed, right_gate)) * matmul(normed, right_weight)).astype(jnp.bfloat16)
    triangle = jnp.einsum('ikc,jkc->ijc', left_proj.astype(jnp.float32), right_proj.astype(jnp.float32), precision=lax.Precision.HIGHEST)
    onormed = layer_norm(triangle, tri_gain, tri_bias).astype(jnp.bfloat16)
    projected = matmul(onormed, out_weight)
    return (jax.nn.sigmoid(matmul(normed, out_gate)) * projected).astype(jnp.bfloat16)
```

```python
import jax
import jax.numpy as jnp
from jax import lax
from jax.sharding import Mesh, PartitionSpec as P

F32 = jnp.float32
BF16 = jnp.bfloat16
CHIPS = ("x", "z", "ylo")
RES = CHIPS + ("core",)


def layer_norm(values, gain, bias):
    values = values.astype(F32)
    row_mean = jnp.mean(values, -1, keepdims=True)
    centred = values - row_mean
    row_var = jnp.mean(centred * centred, -1, keepdims=True)
    return centred * lax.rsqrt(row_var + 1e-05) * gain + bias


def split2(values):
    high = values.astype(BF16)
    low = (values - high.astype(F32)).astype(BF16)
    return high, low


def body(
    pair,
    norm_gain,
    norm_bias,
    left_weight,
    left_gate,
    right_weight,
    right_gate,
    tri_gain,
    tri_bias,
    out_weight,
    out_gate,
):
    rows, tokens, channels = pair.shape
    own = left_weight.shape[1]
    me = lax.axis_index("yhi")
    swap = [(0, 1), (1, 0)]

    scaled = tri_gain[:, None] * out_weight.astype(F32)
    scaled_hi, scaled_lo = split2(scaled)
    gain_sum = jnp.sum(scaled, 0)
    bias_sum = jnp.sum(tri_bias[:, None] * out_weight.astype(F32), 0)
    sums = jnp.stack([gain_sum, bias_sum]).reshape(2, 2, own)
    sums_mine = lax.dynamic_index_in_dim(sums, me, 1, False)
    sums_other = lax.ppermute(lax.dynamic_index_in_dim(sums, 1 - me, 1, False), "yhi", swap)

    normed = layer_norm(pair, norm_gain, norm_bias).astype(BF16).reshape(-1, channels)
    weights = jnp.concatenate([left_gate, left_weight, right_gate, right_weight], 1)
    pre = lax.dot_general(weights, normed, (((0,), (1,)), ((), ())), preferred_element_type=F32)
    left = (jax.nn.sigmoid(pre[:own]) * pre[own : 2 * own]).astype(BF16)
    right = (jax.nn.sigmoid(pre[2 * own : 3 * own]) * pre[3 * own :]).astype(BF16)
    gate_value = jax.nn.sigmoid(
        lax.dot_general(out_gate, normed, (((0,), (1,)), ((), ())), preferred_element_type=F32)
    )

    sent = jnp.stack([left, right], 1).reshape(own, 2 * rows, tokens)
    got = lax.all_to_all(sent, CHIPS, 0, 0, tiled=True)
    left_all = got[:, :rows].reshape(-1, tokens)
    right_all = lax.all_gather(got[:, rows:], "core", axis=1, tiled=True).reshape(-1, tokens)
    triangle = lax.dot_general(
        left_all, right_all, (((1,), (1,)), ((), ())), preferred_element_type=F32
    ).astype(BF16)
    tri = lax.all_to_all(triangle.reshape(own, rows, tokens), CHIPS, 0, 0, tiled=True)
    tri = tri.reshape(own, -1)

    wide = tri.astype(F32)
    mean_mine = jnp.mean(wide, 0, keepdims=True)
    centred = wide - mean_mine
    square_mine = jnp.sum(centred * centred, 0, keepdims=True)
    part = lax.dot_general(
        jnp.concatenate([scaled_hi, scaled_lo], 0),
        jnp.concatenate([tri, tri], 0),
        (((0,), (0,)), ((), ())),
        preferred_element_type=F32,
    )
    part = part - gain_sum[:, None] * mean_mine
    part = part.reshape(2, own, -1)
    part_mine = lax.dynamic_index_in_dim(part, me, 0, False)
    part_other = lax.dynamic_index_in_dim(part, 1 - me, 0, False).astype(BF16)
    payload = jnp.concatenate([part_other, *split2(mean_mine), *split2(square_mine)], 0)
    payload = lax.ppermute(payload, "yhi", swap).astype(F32)

    mean_other = payload[own : own + 1] + payload[own + 1 : own + 2]
    square_other = payload[own + 2 : own + 3] + payload[own + 3 : own + 4]
    mean = 0.5 * (mean_mine + mean_other)
    half = 0.5 * (mean_mine - mean_other)
    var = (square_mine + square_other) / (2 * own) + half * half
    lean = (sums_mine[0] - sums_other[0])[:, None] * half
    projected = (part_mine + payload[:own] + lean) * lax.rsqrt(var + 1e-05)
    projected = projected + (sums_mine[1] + sums_other[1])[:, None]
    updated = (gate_value * projected).astype(BF16)
    return updated.T.reshape(rows, tokens, own)


def solution(mesh):
    fine = Mesh(mesh.devices.reshape(4, 8, 2, 2, 2), RES + ("yhi",))
    placed = (
        P(RES, None, None),
        P(),
        P(),
        P(None, "yhi"),
        P(None, "yhi"),
        P(None, "yhi"),
        P(None, "yhi"),
        P("yhi"),
        P("yhi"),
        P("yhi", None),
        P(None, "yhi"),
    )
    return jax.shard_map(
        body, mesh=fine, in_specs=placed, out_specs=P(RES, None, "yhi"), check_vma=False
    )
```

```python
import jax
import jax.numpy as jnp
from jax import lax
from jax.experimental import pallas as pl
from jax.experimental.pallas import tpu as pltpu
from jax.sharding import Mesh, PartitionSpec as P

F32 = jnp.float32
BF16 = jnp.bfloat16
CHIPS = ("x", "z", "ylo")
RES = CHIPS + ("core",)
EPS = 1e-05


def project_kernel(pair_ref, gain_ref, bias_ref, weight_ref, sent_ref, gate_ref):
    own = gate_ref.shape[1]
    values = pair_ref[0].astype(F32)
    centred = values - jnp.mean(values, -1, keepdims=True)
    row_var = jnp.mean(centred * centred, -1, keepdims=True)
    normed = (centred * lax.rsqrt(row_var + EPS) * gain_ref[...] + bias_ref[...]).astype(BF16)
    pre = lax.dot_general(
        weight_ref[...], normed, (((1,), (1,)), ((), ())), preferred_element_type=F32
    )
    left = jax.nn.sigmoid(pre[:own]) * pre[own : 2 * own]
    right = jax.nn.sigmoid(pre[2 * own : 3 * own]) * pre[3 * own : 4 * own]
    sent_ref[0, 0] = left.astype(BF16)
    sent_ref[1, 0] = right.astype(BF16)
    gate_ref[0] = jax.nn.sigmoid(pre[4 * own :])


def finish_kernel(tri_ref, gate_ref, weight_ref, gain_ref, bias_ref, out_ref):
    values = tri_ref[0].astype(F32)
    centred = values - jnp.mean(values, 0, keepdims=True)
    var = jnp.mean(centred * centred, 0, keepdims=True)
    onormed = (centred * lax.rsqrt(var + EPS) * gain_ref[...] + bias_ref[...]).astype(BF16)
    projected = jnp.dot(weight_ref[...], onormed, preferred_element_type=F32)
    out_ref[0] = (gate_ref[0] * projected).astype(BF16)


def whole(shape):
    return pl.BlockSpec(shape, lambda i: (0,) * len(shape))


def body(
    pair,
    norm_gain,
    norm_bias,
    left_weight,
    left_gate,
    right_weight,
    right_gate,
    tri_gain,
    tri_bias,
    out_weight,
    out_gate,
):
    rows, tokens, channels = pair.shape
    own = left_weight.shape[1]
    me = lax.axis_index("yhi")
    swap = [(0, 1), (1, 0)]

    columns = out_weight.T.reshape(2, own, own)
    extra = jnp.stack([tri_gain, tri_bias])
    mine = lax.dynamic_index_in_dim(columns, me, 0, False).astype(F32)
    theirs = lax.dynamic_index_in_dim(columns, 1 - me, 0, False).astype(F32)
    mine = jnp.concatenate([mine, extra], 0)
    other = lax.ppermute(jnp.concatenate([theirs, extra], 0), "yhi", swap)
    table = jnp.where(
        me == 0, jnp.concatenate([mine, other], 1), jnp.concatenate([other, mine], 1)
    )

    weights = jnp.concatenate(
        [left_gate.T, left_weight.T, right_gate.T, right_weight.T, out_gate.T], 0
    )
    sent, gate_value = pl.pallas_call(
        project_kernel,
        grid=(rows,),
        in_specs=[
            pl.BlockSpec((1, tokens, channels), lambda i: (i, 0, 0)),
            whole((1, channels)),
            whole((1, channels)),
            whole(weights.shape),
        ],
        out_specs=[
            pl.BlockSpec((2, 1, own, tokens), lambda i: (0, i, 0, 0)),
            pl.BlockSpec((1, own, tokens), lambda i: (i, 0, 0)),
        ],
        out_shape=[
            jax.ShapeDtypeStruct((2, rows, own, tokens), BF16),
            jax.ShapeDtypeStruct((rows, own, tokens), F32),
        ],
        name="project",
    )(pair, norm_gain[None], norm_bias[None], weights)

    sent = sent.reshape(2 * rows, own, tokens).swapaxes(0, 1)
    got = lax.all_to_all(sent, CHIPS, 0, 0, tiled=True)
    left_all = got[:, :rows].reshape(-1, tokens)
    right_all = lax.all_gather(got[:, rows:], "core", axis=1, tiled=True).reshape(-1, tokens)
    triangle = lax.dot_general(
        left_all, right_all, (((1,), (1,)), ((), ())), preferred_element_type=F32
    ).astype(BF16)
    triangle = jnp.broadcast_to(triangle.reshape(1, own, rows, tokens), (2, own, rows, tokens))
    tri = lax.all_to_all(
        triangle.reshape(2 * own, rows, tokens), ("yhi",) + CHIPS, 0, 0, tiled=True
    ).swapaxes(0, 1)

    updated = pl.pallas_call(
        finish_kernel,
        grid=(rows,),
        in_specs=[
            pl.BlockSpec((1, channels, tokens), lambda i: (i, 0, 0)),
            pl.BlockSpec((1, own, tokens), lambda i: (i, 0, 0)),
            whole((own, channels)),
            whole((channels, 1)),
            whole((channels, 1)),
        ],
        out_specs=pl.BlockSpec((1, own, tokens), lambda i: (i, 0, 0)),
        out_shape=jax.ShapeDtypeStruct((rows, own, tokens), BF16),
        name="finish",
    )(
        tri,
        gate_value,
        table[:own].astype(BF16),
        table[own].reshape(-1, 1),
        table[own + 1].reshape(-1, 1),
    )
    return updated.swapaxes(1, 2)


def solution(mesh):
    fine = Mesh(mesh.devices.reshape(4, 8, 2, 2, 2), RES + ("yhi",))
    placed = (
        P(RES, None, None),
        P(),
        P(),
        P(None, "yhi"),
        P(None, "yhi"),
        P(None, "yhi"),
        P(None, "yhi"),
        P("yhi"),
        P("yhi"),
        P("yhi", None),
        P(None, "yhi"),
    )
    return jax.shard_map(
        body, mesh=fine, in_specs=placed, out_specs=P(RES, None, "yhi"), check_vma=False
    )
```

```python
import jax
import jax.numpy as jnp
from jax import lax
from jax.sharding import Mesh, PartitionSpec as P

F32 = jnp.float32
BF16 = jnp.bfloat16
CHIPS = ("x", "z", "ylo")
RES = CHIPS + ("core",)
EPS = 1e-05
SWAP = [(0, 1), (1, 0)]


def normalise(values, axis, gain, bias):
    centred = values - jnp.mean(values, axis, keepdims=True)
    var = jnp.mean(centred * centred, axis, keepdims=True)
    return (centred * lax.rsqrt(var + EPS) * gain[:, None] + bias[:, None]).astype(BF16)


def split3(values):
    high = values.astype(BF16)
    rest = values - high.astype(F32)
    middle = rest.astype(BF16)
    return jnp.stack([high, middle, (rest - middle.astype(F32)).astype(BF16)])


def per_row(matrix, values):
    matrix = jnp.broadcast_to(matrix, values.shape[:1] + matrix.shape)
    return lax.dot_general(matrix, values, (((2,), (1,)), ((0,), (0,))), preferred_element_type=F32)


def body(
    pair,
    norm_gain,
    norm_bias,
    left_weight,
    left_gate,
    right_weight,
    right_gate,
    tri_gain,
    tri_bias,
    out_weight,
    out_gate,
):
    rows, tokens, channels = pair.shape
    own = left_weight.shape[1]

    eye = jnp.broadcast_to(jnp.eye(channels, dtype=BF16), (rows, channels, channels))
    wide = lax.dot_general(eye, pair, (((2,), (2,)), ((0,), (0,))), preferred_element_type=F32)
    normed = normalise(wide, 1, norm_gain, norm_bias)
    weights = [left_gate.T, left_weight.T, right_gate.T, right_weight.T]
    pre = per_row(jnp.concatenate(weights, 0), normed)
    left = (jax.nn.sigmoid(pre[:, :own]) * pre[:, own : 2 * own]).astype(BF16)
    right = (jax.nn.sigmoid(pre[:, 2 * own : 3 * own]) * pre[:, 3 * own :]).astype(BF16)
    sent = jnp.concatenate([left, right], 0).transpose(1, 0, 2)
    first = lax.axis_index("core") == 0
    half = lax.axis_index("yhi") * own
    sent, first, half = lax.optimization_barrier((sent, first, half))

    got = lax.all_to_all(sent, CHIPS, 0, 0, tiled=True)
    got, out_weight, tri_gain, tri_bias = lax.optimization_barrier(
        (got, out_weight, tri_gain, tri_bias)
    )
    right_own = got[:, rows:]
    right_other = lax.ppermute(right_own, "core", SWAP)
    extra = split3(jnp.stack([tri_gain, tri_bias]))
    extra = jnp.concatenate([out_weight.reshape(-1), extra.reshape(-1)])
    extra = jnp.pad(extra, (0, -extra.size % (rows * tokens))).reshape(-1, rows, tokens)
    right_other, extra = lax.optimization_barrier((right_other, extra))
    right_all = jnp.where(
        first,
        jnp.concatenate([right_own, right_other], 1),
        jnp.concatenate([right_other, right_own], 1),
    )
    triangle = lax.dot_general(
        got[:, :rows].reshape(-1, tokens),
        right_all.reshape(-1, tokens),
        (((1,), (1,)), ((), ())),
        preferred_element_type=F32,
    ).astype(BF16)

    tri = lax.all_to_all(triangle.reshape(own, rows, tokens), CHIPS, 0, 0, tiled=True)
    payload = lax.ppermute(jnp.concatenate([tri, extra], 0), "yhi", SWAP)
    gate_value = jax.nn.sigmoid(per_row(out_gate.T, normed))

    tail = payload[own:].reshape(-1)
    weight_other = tail[: out_weight.size].reshape(out_weight.shape)
    scales_other = tail[out_weight.size : out_weight.size + 6 * own].reshape(3, 2, own)
    scales = jnp.concatenate(
        [jnp.stack([tri_gain, tri_bias]), jnp.sum(scales_other.astype(F32), 0)], 1
    )
    weight = jnp.concatenate([out_weight, weight_other], 0)
    weight = lax.dynamic_slice_in_dim(weight, half, own, 1)
    wide = jnp.concatenate([tri, payload[:own]], 0).astype(F32).reshape(2 * own, -1)
    onormed = normalise(wide, 0, scales[0], scales[1])
    projected = lax.dot_general(
        weight, onormed, (((0,), (0,)), ((), ())), preferred_element_type=F32
    )
    gate_value = gate_value.transpose(1, 0, 2).reshape(own, -1)
    updated = (gate_value * projected).astype(BF16)
    return updated.reshape(own, rows, tokens).transpose(1, 2, 0)


def solution(mesh):
    fine = Mesh(mesh.devices.reshape(4, 8, 2, 2, 2), RES + ("yhi",))
    placed = (
        P(RES, None, None),
        P(),
        P(),
        P(None, "yhi"),
        P(None, "yhi"),
        P(None, "yhi"),
        P(None, "yhi"),
        P("yhi"),
        P("yhi"),
        P("yhi", None),
        P(None, "yhi"),
    )
    return jax.shard_map(
        body, mesh=fine, in_specs=placed, out_specs=P(RES, None, "yhi"), check_vma=False
    )
```

```python
import jax
import jax.numpy as jnp
from jax import lax
from jax.experimental import pallas as pl
from jax.experimental.pallas import tpu as pltpu
from jax.sharding import Mesh, PartitionSpec as P

F32 = jnp.float32
BF16 = jnp.bfloat16
CHIPS = ("x", "z", "ylo")
RES = CHIPS + ("core",)
EPS = 1e-05
SWAP = [(0, 1), (1, 0)]


def normalise(values, axis, gain, bias):
    centred = values - jnp.mean(values, axis, keepdims=True)
    var = jnp.mean(centred * centred, axis, keepdims=True)
    return (centred * lax.rsqrt(var + EPS) * gain[:, None] + bias[:, None]).astype(BF16)


def split3(values):
    high = values.astype(BF16)
    rest = values - high.astype(F32)
    middle = rest.astype(BF16)
    return jnp.stack([high, middle, (rest - middle.astype(F32)).astype(BF16)])


def per_row(matrix, values):
    matrix = jnp.broadcast_to(matrix, values.shape[:1] + matrix.shape)
    return lax.dot_general(matrix, values, (((2,), (1,)), ((0,), (0,))), preferred_element_type=F32)


def pack(weight, scales):
    pieces = jnp.pad(split3(scales).transpose(1, 0, 2).reshape(6, -1), ((0, 2), (0, 0)))
    beside = jnp.concatenate([pieces[None], jnp.zeros((7,) + pieces.shape, BF16)], 0)
    tiles = jnp.concatenate([weight.reshape(8, 8, -1), beside], 2)
    return tiles.reshape(2, 4, 8, -1).transpose(0, 2, 1, 3).reshape(16, -1)


def unpack(block):
    tiles = [block[8 * g : 8 * g + 8, 128 * t : 128 * t + 128] for g in range(2) for t in range(4)]
    half = tiles[0].shape[1] // 2
    columns = tiles[0].astype(F32).T[half:]
    gain = columns[:, 0:1] + columns[:, 1:2] + columns[:, 2:3]
    bias = columns[:, 3:4] + columns[:, 4:5] + columns[:, 5:6]
    return jnp.concatenate([tile[:, :half] for tile in tiles], 0), gain, bias


def finish_kernel(mine_ref, other_ref, gate_ref, out_ref, done, sems):
    rows, own, _ = gate_ref.shape
    size = rows * own
    weight, gain, bias = unpack(mine_ref[size:])
    weight_other, gain_other, bias_other = unpack(other_ref[size:])
    weight = jnp.concatenate([weight, weight_other], 1)
    copies = [pltpu.make_async_copy(done.at[i], out_ref.at[i], sems.at[i]) for i in range(rows)]
    width = 512
    for i in range(rows):
        for part in range(done.shape[2] // width):
            at = slice(part * width, (part + 1) * width)
            mine = mine_ref[i * own : (i + 1) * own, at].astype(F32)
            other = other_ref[i * own : (i + 1) * own, at].astype(F32)
            mean = (jnp.sum(mine, 0, keepdims=True) + jnp.sum(other, 0, keepdims=True)) / (2 * own)
            mine, other = mine - mean, other - mean
            square = jnp.sum(mine * mine + other * other, 0, keepdims=True)
            root = lax.rsqrt(square / (2 * own) + EPS)
            onormed = [mine * root * gain + bias, other * root * gain_other + bias_other]
            onormed = jnp.concatenate(onormed, 0).astype(BF16)
            projected = jnp.dot(weight, onormed, preferred_element_type=F32)
            done[i, :, at] = (gate_ref[i, :, at] * projected).astype(BF16)
        if 'each' == "each":
            copies[i].start()
        elif i % 2 == 1:
            copies[i - 1].start()
            copies[i].start()
    for copy in copies:
        copy.wait()


def finish(mine, other, gate_value):
    rows, own, tokens = gate_value.shape
    operands = [pltpu.with_memory_space_constraint(a, pltpu.VMEM) for a in (mine, other, gate_value)]
    return pl.pallas_call(
        finish_kernel,
        in_specs=[pl.BlockSpec(memory_space=pltpu.VMEM)] * 3,
        out_specs=pl.BlockSpec(memory_space=pl.ANY),
        out_shape=jax.ShapeDtypeStruct((rows, own, tokens), BF16),
        scratch_shapes=[pltpu.VMEM((rows, own, tokens), BF16), pltpu.SemaphoreType.DMA((rows,))],
        name="finish",
    )(*operands)


def body(
    pair,
    norm_gain,
    norm_bias,
    left_weight,
    left_gate,
    right_weight,
    right_gate,
    tri_gain,
    tri_bias,
    out_weight,
    out_gate,
):
    rows, tokens, channels = pair.shape
    own = left_weight.shape[1]

    eye = jnp.broadcast_to(jnp.eye(channels, dtype=BF16), (rows, channels, channels))
    wide = lax.dot_general(eye, pair, (((2,), (2,)), ((0,), (0,))), preferred_element_type=F32)
    normed = normalise(wide, 1, norm_gain, norm_bias)
    weights = [left_gate.T, left_weight.T, right_gate.T, right_weight.T]
    pre = per_row(jnp.concatenate(weights, 0), normed)
    left = (jax.nn.sigmoid(pre[:, :own]) * pre[:, own : 2 * own]).astype(BF16)
    right = (jax.nn.sigmoid(pre[:, 2 * own : 3 * own]) * pre[:, 3 * own :]).astype(BF16)
    sent = jnp.concatenate([left, right], 0).transpose(1, 0, 2)
    first = lax.axis_index("core") == 0
    low = lax.axis_index("yhi") == 0
    sent, first, low = lax.optimization_barrier((sent, first, low))

    got = lax.all_to_all(sent, CHIPS, 0, 0, tiled=True)
    got, out_weight, tri_gain, tri_bias = lax.optimization_barrier(
        (got, out_weight, tri_gain, tri_bias)
    )
    right_own = got[:, rows:]
    right_other = lax.ppermute(right_own, "core", SWAP)
    columns = out_weight.T.reshape(2, own, own)
    scales = jnp.stack([tri_gain, tri_bias])
    extra = pack(jnp.where(low, columns[1], columns[0]), scales)
    extra_own = pack(jnp.where(low, columns[0], columns[1]), scales)
    right_other, extra, extra_own = lax.optimization_barrier((right_other, extra, extra_own))
    right_all = jnp.where(
        first,
        jnp.concatenate([right_own, right_other], 1),
        jnp.concatenate([right_other, right_own], 1),
    )
    triangle = lax.dot_general(
        got[:, :rows].reshape(-1, tokens),
        right_all.reshape(-1, tokens),
        (((1,), (1,)), ((), ())),
        preferred_element_type=F32,
    ).astype(BF16)

    tri = lax.all_to_all(triangle.reshape(own, rows, tokens), CHIPS, 0, 0, tiled=True)
    tri = tri.transpose(1, 0, 2).reshape(-1, tokens)
    other = lax.ppermute(jnp.concatenate([tri, extra], 0), "yhi", SWAP)
    gate_value = jax.nn.sigmoid(per_row(out_gate.T, normed))
    updated = finish(jnp.concatenate([tri, extra_own], 0), other, gate_value)
    return updated.transpose(0, 2, 1)


def solution(mesh):
    fine = Mesh(mesh.devices.reshape(4, 8, 2, 2, 2), RES + ("yhi",))
    placed = (
        P(RES, None, None),
        P(),
        P(),
        P(None, "yhi"),
        P(None, "yhi"),
        P(None, "yhi"),
        P(None, "yhi"),
        P("yhi"),
        P("yhi"),
        P("yhi", None),
        P(None, "yhi"),
    )
    return jax.shard_map(
        body, mesh=fine, in_specs=placed, out_specs=P(RES, None, "yhi"), check_vma=False
    )
```

```python
import jax
import jax.numpy as jnp
from jax import lax
from jax.experimental import pallas as pl
from jax.experimental.pallas import tpu as pltpu
from jax.sharding import Mesh, PartitionSpec as P

F32 = jnp.float32
BF16 = jnp.bfloat16
CHIPS = ("x", "z", "ylo")
RES = CHIPS + ("core",)
EPS = 1e-05
SWAP = [(0, 1), (1, 0)]


def split3(values):
    high = values.astype(BF16)
    rest = values - high.astype(F32)
    middle = rest.astype(BF16)
    return [high, middle, (rest - middle.astype(F32)).astype(BF16)]


def per_row(matrix, values):
    matrix = jnp.broadcast_to(matrix, values.shape[:1] + matrix.shape)
    return lax.dot_general(matrix, values, (((2,), (1,)), ((0,), (0,))), preferred_element_type=F32)


def sigmoid(values):
    return 0.5 * jnp.tanh(0.5 * values) + 0.5


def pack(weight, scales):
    pieces = [piece.astype(F32) for row in scales for piece in split3(row)]
    beside = jnp.concatenate(pieces + [jnp.zeros_like(pieces[0])] * 2, 0)
    tiles = [
        jnp.concatenate([weight[8 * g : 8 * g + 8], beside if g == 0 else jnp.zeros_like(beside)], 1)
        for g in range(8)
    ]
    halves = [jnp.concatenate(tiles[4 * h : 4 * h + 4], 1) for h in range(2)]
    return jnp.concatenate(halves, 0).astype(BF16)


def project_kernel(*refs):
    pair_ref, scale_refs, weight_refs, out_weight_ref = refs[0], refs[1:5], refs[5:9], refs[9]
    sent_ref, normed_ref, extra_ref, extra_own_ref = refs[10:14]
    pair_buf, scale_buf, tri_buf, weight_buf, out_weight_buf, sem, sems = refs[14:]
    rows, tokens, channels = pair_buf.shape
    own = weight_refs[0].shape[0]
    load = pltpu.make_async_copy(pair_ref, pair_buf, sem)
    load.start()
    copies = [pltpu.make_async_copy(out_weight_ref, out_weight_buf, sems.at[8])]
    for n in range(4):
        place = (scale_buf, tri_buf)[n // 2].at[pl.ds(8 * (n % 2), 1)]
        copies.append(pltpu.make_async_copy(scale_refs[n], place, sems.at[n]))
        place = weight_buf.at[pl.ds(own * n, own)]
        copies.append(pltpu.make_async_copy(weight_refs[n], place, sems.at[4 + n]))
    for copy in copies:
        copy.start()
    for copy in copies + [load]:
        copy.wait()

    scales = scale_buf[...].T
    values = pair_buf[...].reshape(rows * tokens, channels).T.astype(F32)
    centred = values - jnp.mean(values, 0, keepdims=True)
    var = jnp.mean(centred * centred, 0, keepdims=True)
    normed = centred * lax.rsqrt(var + EPS) * scales[:, 0:1] + scales[:, 8:9]
    normed = normed.astype(BF16)
    pre = jnp.dot(weight_buf[...], normed, preferred_element_type=F32)
    for i in range(rows):
        at = slice(i * tokens, (i + 1) * tokens)
        normed_ref[i] = normed[:, at]
        sent_ref[i] = (sigmoid(pre[:own, at]) * pre[own : 2 * own, at]).astype(BF16)
        right = sigmoid(pre[2 * own : 3 * own, at]) * pre[3 * own :, at]
        sent_ref[rows + i] = right.astype(BF16)

    tri = [tri_buf[0:1], tri_buf[8:9]]
    columns = out_weight_buf[...].astype(F32).T
    low = lax.axis_index("yhi") == 0
    extra_ref[...] = pack(jnp.where(low, columns[own:], columns[:own]), tri)
    extra_own_ref[...] = pack(jnp.where(low, columns[:own], columns[own:]), tri)


def project(pair, scales, weights, out_weight):
    rows, tokens, channels = pair.shape
    own = weights[0].shape[0]
    return pl.pallas_call(
        project_kernel,
        in_specs=[pl.BlockSpec(memory_space=pl.ANY)] * 10,
        out_specs=[pl.BlockSpec(memory_space=pltpu.VMEM)] * 4,
        out_shape=[
            pltpu.VMEM((2 * rows, own, tokens), BF16),
            pltpu.VMEM((rows, channels, tokens), BF16),
            pltpu.VMEM((16, 512), BF16),
            pltpu.VMEM((16, 512), BF16),
        ],
        scratch_shapes=[
            pltpu.VMEM((rows, tokens, channels), BF16),
            pltpu.VMEM((16, channels), F32),
            pltpu.VMEM((16, own), F32),
            pltpu.VMEM((4 * own, channels), BF16),
            pltpu.VMEM((own, channels), BF16),
            pltpu.SemaphoreType.DMA,
            pltpu.SemaphoreType.DMA((9,)),
        ],
        name="project",
    )(
        *[
            pltpu.with_memory_space_constraint(a, pltpu.HBM)
            for a in [pair] + [v[None] for v in scales] + weights + [out_weight]
        ]
    )


def unpack(block):
    block = block.astype(F32)
    tiles = [block[8 * g : 8 * g + 8, 128 * t : 128 * t + 128] for g in range(2) for t in range(4)]
    half = tiles[0].shape[1] // 2
    columns = tiles[0].T[half:]
    gain = columns[:, 0:1] + columns[:, 1:2] + columns[:, 2:3]
    bias = columns[:, 3:4] + columns[:, 4:5] + columns[:, 5:6]
    return jnp.concatenate([tile[:, :half] for tile in tiles], 0).astype(BF16), gain, bias


def finish_kernel(mine_ref, other_ref, gate_ref, out_ref, done, sems):
    rows, own, _ = gate_ref.shape
    size = rows * own
    weight, gain, bias = unpack(mine_ref[size:])
    weight_other, gain_other, bias_other = unpack(other_ref[size:])
    weight = jnp.concatenate([weight, weight_other], 1)
    copies = [pltpu.make_async_copy(done.at[i], out_ref.at[i], sems.at[i]) for i in range(rows)]
    width = 512
    for i in range(rows):
        for part in range(done.shape[2] // width):
            at = slice(part * width, (part + 1) * width)
            mine = mine_ref[i * own : (i + 1) * own, at].astype(F32)
            other = other_ref[i * own : (i + 1) * own, at].astype(F32)
            mean = (jnp.sum(mine, 0, keepdims=True) + jnp.sum(other, 0, keepdims=True)) / (2 * own)
            mine, other = mine - mean, other - mean
            square = jnp.sum(mine * mine + other * other, 0, keepdims=True)
            root = lax.rsqrt(square / (2 * own) + EPS)
            onormed = [mine * root * gain + bias, other * root * gain_other + bias_other]
            onormed = jnp.concatenate(onormed, 0).astype(BF16)
            projected = jnp.dot(weight, onormed, preferred_element_type=F32)
            done[i, :, at] = (gate_ref[i, :, at] * projected).astype(BF16)
        if 'each' == "each":
            copies[i].start()
        elif i % 2 == 1:
            copies[i - 1].start()
            copies[i].start()
    for copy in copies:
        copy.wait()


def finish(mine, other, gate_value):
    rows, own, tokens = gate_value.shape
    operands = [pltpu.with_memory_space_constraint(a, pltpu.VMEM) for a in (mine, other, gate_value)]
    return pl.pallas_call(
        finish_kernel,
        in_specs=[pl.BlockSpec(memory_space=pltpu.VMEM)] * 3,
        out_specs=pl.BlockSpec(memory_space=pl.ANY),
        out_shape=jax.ShapeDtypeStruct((rows, own, tokens), BF16),
        scratch_shapes=[pltpu.VMEM((rows, own, tokens), BF16), pltpu.SemaphoreType.DMA((rows,))],
        name="finish",
    )(*operands)


def body(
    pair,
    norm_gain,
    norm_bias,
    left_weight,
    left_gate,
    right_weight,
    right_gate,
    tri_gain,
    tri_bias,
    out_weight,
    out_gate,
):
    rows, tokens, channels = pair.shape
    own = left_weight.shape[1]

    sent, normed, extra, extra_own = project(
        pair,
        [norm_gain, norm_bias, tri_gain, tri_bias],
        [left_gate.T, left_weight.T, right_gate.T, right_weight.T],
        out_weight,
    )
    sent = sent.transpose(1, 0, 2)
    first = lax.axis_index("core") == 0
    sent, first = lax.optimization_barrier((sent, first))

    got = lax.all_to_all(sent, CHIPS, 0, 0, tiled=True)
    right_own = got[:, rows:]
    right_other = lax.ppermute(right_own, "core", SWAP)
    right_all = jnp.where(
        first,
        jnp.concatenate([right_own, right_other], 1),
        jnp.concatenate([right_other, right_own], 1),
    )
    triangle = lax.dot_general(
        got[:, :rows].reshape(-1, tokens),
        right_all.reshape(-1, tokens),
        (((1,), (1,)), ((), ())),
        preferred_element_type=F32,
    ).astype(BF16)

    tri = lax.all_to_all(triangle.reshape(own, rows, tokens), CHIPS, 0, 0, tiled=True)
    tri = tri.transpose(1, 0, 2).reshape(-1, tokens)
    other = lax.ppermute(jnp.concatenate([tri, extra], 0), "yhi", SWAP)
    gate_value = jax.nn.sigmoid(per_row(out_gate.T, normed))
    updated = finish(jnp.concatenate([tri, extra_own], 0), other, gate_value)
    return updated.transpose(0, 2, 1)


def solution(mesh):
    fine = Mesh(mesh.devices.reshape(4, 8, 2, 2, 2), RES + ("yhi",))
    placed = (
        P(RES, None, None),
        P(),
        P(),
        P(None, "yhi"),
        P(None, "yhi"),
        P(None, "yhi"),
        P(None, "yhi"),
        P("yhi"),
        P("yhi"),
        P("yhi", None),
        P(None, "yhi"),
    )
    return jax.shard_map(
        body, mesh=fine, in_specs=placed, out_specs=P(RES, None, "yhi"), check_vma=False
    )
```

```python
import jax
import jax.numpy as jnp
from jax import lax
from jax.experimental import pallas as pl
from jax.experimental.pallas import tpu as pltpu
from jax.sharding import Mesh, PartitionSpec as P

F32 = jnp.float32
BF16 = jnp.bfloat16
CHIPS = ("x", "z", "ylo")
RES = CHIPS + ("core",)
EPS = 1e-05
SWAP = [(0, 1), (1, 0)]


def split3(values):
    high = values.astype(BF16)
    rest = values - high.astype(F32)
    middle = rest.astype(BF16)
    return [high, middle, (rest - middle.astype(F32)).astype(BF16)]


def per_row(matrix, values):
    matrix = jnp.broadcast_to(matrix, values.shape[:1] + matrix.shape)
    return lax.dot_general(matrix, values, (((2,), (1,)), ((0,), (0,))), preferred_element_type=F32)


def sigmoid(values):
    return 0.5 * jnp.tanh(0.5 * values) + 0.5


def pack(columns):
    return jnp.concatenate([columns[16 * t : 16 * t + 16] for t in range(4)], 1).astype(BF16)


def unpack(block):
    return jnp.concatenate([block[:, 128 * t : 128 * t + 128] for t in range(4)], 0)


def project_kernel(*refs):
    pair_ref, scale_refs, weight_refs, out_weight_ref = refs[0], refs[1:5], refs[5:9], refs[9]
    sent_ref, normed_ref, extra_ref, extra_own_ref = refs[10:14]
    pair_buf, scale_buf, tri_buf, weight_buf, out_weight_buf, sem, sems = refs[14:]
    rows, tokens, channels = pair_buf.shape
    own = weight_refs[0].shape[0]
    load = pltpu.make_async_copy(pair_ref, pair_buf, sem)
    load.start()
    copies = [pltpu.make_async_copy(out_weight_ref, out_weight_buf, sems.at[8])]
    for n in range(4):
        place = (scale_buf, tri_buf)[n // 2].at[pl.ds(8 * (n % 2), 1)]
        copies.append(pltpu.make_async_copy(scale_refs[n], place, sems.at[n]))
        place = weight_buf.at[pl.ds(own * n, own)]
        copies.append(pltpu.make_async_copy(weight_refs[n], place, sems.at[4 + n]))
    for copy in copies:
        copy.start()
    for copy in copies + [load]:
        copy.wait()

    scales = scale_buf[...].T
    values = pair_buf[...].reshape(rows * tokens, channels).T.astype(F32)
    centred = values - jnp.mean(values, 0, keepdims=True)
    var = jnp.mean(centred * centred, 0, keepdims=True)
    normed = centred * lax.rsqrt(var + EPS) * scales[:, 0:1] + scales[:, 8:9]
    normed = normed.astype(BF16)
    pre = jnp.dot(weight_buf[...], normed, preferred_element_type=F32)
    for i in range(rows):
        at = slice(i * tokens, (i + 1) * tokens)
        normed_ref[i] = normed[:, at]
        sent_ref[rows + i] = (sigmoid(pre[:own, at]) * pre[own : 2 * own, at]).astype(BF16)
        right = sigmoid(pre[2 * own : 3 * own, at]) * pre[3 * own :, at]
        sent_ref[i] = right.astype(BF16)

    pieces = [piece.astype(F32) for n in (0, 8) for piece in split3(tri_buf[n : n + 1])]
    pieces = jnp.concatenate(pieces + [jnp.zeros_like(pieces[0])] * 2, 0).T
    blank = jnp.zeros((own, channels - own - 8), F32)
    columns = out_weight_buf[...].astype(F32).T
    low = lax.axis_index("yhi") == 0
    mine = jnp.where(low, columns[:own], columns[own:])
    theirs = jnp.where(low, columns[own:], columns[:own])
    extra_ref[...] = pack(jnp.concatenate([pieces, blank, theirs], 1))
    extra_own_ref[...] = pack(jnp.concatenate([mine, pieces, blank], 1))


def project(pair, scales, weights, out_weight):
    rows, tokens, channels = pair.shape
    own = weights[0].shape[0]
    return pl.pallas_call(
        project_kernel,
        in_specs=[pl.BlockSpec(memory_space=pl.ANY)] * 10,
        out_specs=[pl.BlockSpec(memory_space=pltpu.VMEM)] * 4,
        out_shape=[
            pltpu.VMEM((2 * rows, own, tokens), BF16),
            pltpu.VMEM((rows, channels, tokens), BF16),
            pltpu.VMEM((16, 512), BF16),
            pltpu.VMEM((16, 512), BF16),
        ],
        scratch_shapes=[
            pltpu.VMEM((rows, tokens, channels), BF16),
            pltpu.VMEM((16, channels), F32),
            pltpu.VMEM((16, own), F32),
            pltpu.VMEM((4 * own, channels), BF16),
            pltpu.VMEM((own, channels), BF16),
            pltpu.SemaphoreType.DMA,
            pltpu.SemaphoreType.DMA((9,)),
        ],
        name="project",
    )(
        *[
            pltpu.with_memory_space_constraint(a, pltpu.HBM)
            for a in [pair] + [v[None] for v in scales] + weights + [out_weight]
        ]
    )


def scales_of(pieces):
    gain = pieces[:, 0:1] + pieces[:, 1:2] + pieces[:, 2:3]
    return gain, pieces[:, 3:4] + pieces[:, 4:5] + pieces[:, 5:6]


def finish_kernel(mine_ref, other_ref, gate_ref, out_ref, done, sems):
    rows, own, _ = gate_ref.shape
    size = rows * own
    columns, columns_other = unpack(mine_ref[size:]), unpack(other_ref[size:])
    lane = lax.broadcasted_iota(jnp.int32, columns.shape, 1)
    weight = jnp.where(lane < own, columns.astype(F32), columns_other.astype(F32)).astype(BF16)
    gain, bias = scales_of(columns[:, own : own + 8].astype(F32))
    gain_other, bias_other = scales_of(columns_other[:, 0:8].astype(F32))
    copies = [pltpu.make_async_copy(done.at[i], out_ref.at[i], sems.at[i]) for i in range(rows)]
    for i in range(rows):
        mine = mine_ref[i * own : (i + 1) * own].astype(F32)
        other = other_ref[i * own : (i + 1) * own].astype(F32)
        mean = (jnp.sum(mine, 0, keepdims=True) + jnp.sum(other, 0, keepdims=True)) / (2 * own)
        mine, other = mine - mean, other - mean
        square = jnp.sum(mine * mine + other * other, 0, keepdims=True)
        root = lax.rsqrt(square / (2 * own) + EPS)
        onormed = [mine * root * gain + bias, other * root * gain_other + bias_other]
        onormed = jnp.concatenate(onormed, 0).astype(BF16)
        projected = jnp.dot(weight, onormed, preferred_element_type=F32)
        done[i] = (gate_ref[i] * projected).astype(BF16)
        copies[i].start()
    for copy in copies:
        copy.wait()


def finish(mine, other, gate_value):
    rows, own, tokens = gate_value.shape
    operands = [pltpu.with_memory_space_constraint(a, pltpu.VMEM) for a in (mine, other, gate_value)]
    return pl.pallas_call(
        finish_kernel,
        in_specs=[pl.BlockSpec(memory_space=pltpu.VMEM)] * 3,
        out_specs=pl.BlockSpec(memory_space=pl.ANY),
        out_shape=jax.ShapeDtypeStruct((rows, own, tokens), BF16),
        scratch_shapes=[pltpu.VMEM((rows, own, tokens), BF16), pltpu.SemaphoreType.DMA((rows,))],
        name="finish",
    )(*operands)


def body(
    pair,
    norm_gain,
    norm_bias,
    left_weight,
    left_gate,
    right_weight,
    right_gate,
    tri_gain,
    tri_bias,
    out_weight,
    out_gate,
):
    rows, tokens, channels = pair.shape
    own = left_weight.shape[1]

    sent, normed, extra, extra_own = project(
        pair,
        [norm_gain, norm_bias, tri_gain, tri_bias],
        [left_gate.T, left_weight.T, right_gate.T, right_weight.T],
        out_weight,
    )
    sent = sent.transpose(1, 0, 2)
    first = lax.axis_index("core") == 0
    sent, first = lax.optimization_barrier((sent, first))

    got = lax.all_to_all(sent, CHIPS, 0, 0, tiled=True)
    right_own, got = lax.optimization_barrier((got[:, :rows], got))
    right_other = lax.ppermute(right_own, "core", SWAP)
    right_all = jnp.where(
        first,
        jnp.concatenate([right_own, right_other], 1),
        jnp.concatenate([right_other, right_own], 1),
    )
    triangle = lax.dot_general(
        got[:, rows:].reshape(-1, tokens),
        right_all.reshape(-1, tokens),
        (((1,), (1,)), ((), ())),
        preferred_element_type=F32,
    ).astype(BF16)

    tri = lax.all_to_all(triangle.reshape(own, rows, tokens), CHIPS, 0, 0, tiled=True)
    tri = tri.transpose(1, 0, 2).reshape(-1, tokens)
    other = lax.ppermute(jnp.concatenate([tri, extra], 0), "yhi", SWAP)
    gate_value = jax.nn.sigmoid(per_row(out_gate.T, normed))
    updated = finish(jnp.concatenate([tri, extra_own], 0), other, gate_value)
    return updated.transpose(0, 2, 1)


def solution(mesh):
    fine = Mesh(mesh.devices.reshape(4, 8, 2, 2, 2), RES + ("yhi",))
    placed = (
        P(RES, None, None),
        P(),
        P(),
        P(None, "yhi"),
        P(None, "yhi"),
        P(None, "yhi"),
        P(None, "yhi"),
        P("yhi"),
        P("yhi"),
        P("yhi", None),
        P(None, "yhi"),
    )
    return jax.shard_map(
        body, mesh=fine, in_specs=placed, out_specs=P(RES, None, "yhi"), check_vma=False
    )
```

```python
import jax
import jax.numpy as jnp
from jax import lax
from jax.experimental import pallas as pl
from jax.experimental.pallas import tpu as pltpu
from jax.sharding import Mesh, PartitionSpec as P

F32 = jnp.float32
BF16 = jnp.bfloat16
CHIPS = ("x", "z", "ylo")
RES = CHIPS + ("core",)
EPS = 1e-05
SWAP = [(0, 1), (1, 0)]


def split3(values):
    high = values.astype(BF16)
    rest = values - high.astype(F32)
    middle = rest.astype(BF16)
    return [high, middle, (rest - middle.astype(F32)).astype(BF16)]


def per_row(matrix, values):
    matrix = jnp.broadcast_to(matrix, values.shape[:1] + matrix.shape)
    return lax.dot_general(matrix, values, (((2,), (1,)), ((0,), (0,))), preferred_element_type=F32)


def sigmoid(values):
    return 0.5 * jnp.tanh(0.5 * values) + 0.5


def pack(columns):
    return jnp.concatenate([columns[16 * t : 16 * t + 16] for t in range(4)], 1).astype(BF16)


def unpack(block):
    return jnp.concatenate([block[:, 128 * t : 128 * t + 128] for t in range(4)], 0)


def project_kernel(*refs):
    pair_ref, scale_refs, weight_refs, out_weight_ref = refs[0], refs[1:5], refs[5:9], refs[9]
    sent_ref, normed_ref, extra_ref, extra_own_ref = refs[10:14]
    pair_buf, scale_buf, tri_buf, weight_buf, out_weight_buf, sem, sems = refs[14:]
    rows, tokens, channels = pair_buf.shape
    own = weight_refs[0].shape[0]
    load = pltpu.make_async_copy(pair_ref, pair_buf, sem)
    load.start()
    copies = [pltpu.make_async_copy(out_weight_ref, out_weight_buf, sems.at[8])]
    for n in range(4):
        place = (scale_buf, tri_buf)[n // 2].at[pl.ds(8 * (n % 2), 1)]
        copies.append(pltpu.make_async_copy(scale_refs[n], place, sems.at[n]))
        place = weight_buf.at[pl.ds(own * n, own)]
        copies.append(pltpu.make_async_copy(weight_refs[n], place, sems.at[4 + n]))
    for copy in copies:
        copy.start()
    for copy in copies + [load]:
        copy.wait()

    scales = scale_buf[...].T
    values = pair_buf[...].reshape(rows * tokens, channels).T.astype(F32)
    centred = values - jnp.mean(values, 0, keepdims=True)
    var = jnp.mean(centred * centred, 0, keepdims=True)
    normed = centred * lax.rsqrt(var + EPS) * scales[:, 0:1] + scales[:, 8:9]
    normed = normed.astype(BF16)
    pre = jnp.dot(weight_buf[...], normed, preferred_element_type=F32)
    left, right = [], []
    for i in range(rows):
        at = slice(i * tokens, (i + 1) * tokens)
        normed_ref[i] = normed[:, at]
        left.append((sigmoid(pre[:own, at]) * pre[own : 2 * own, at]).astype(BF16))
        right.append((sigmoid(pre[2 * own : 3 * own, at]) * pre[3 * own :, at]).astype(BF16))
    sent_ref[...] = jnp.swapaxes(jnp.stack(right + left, 0), 0, 1)

    pieces = [piece.astype(F32) for n in (0, 8) for piece in split3(tri_buf[n : n + 1])]
    pieces = jnp.concatenate(pieces + [jnp.zeros_like(pieces[0])] * 2, 0).T
    blank = jnp.zeros((own, channels - own - 8), F32)
    columns = out_weight_buf[...].astype(F32).T
    low = lax.axis_index("yhi") == 0
    mine = jnp.where(low, columns[:own], columns[own:])
    theirs = jnp.where(low, columns[own:], columns[:own])
    extra_ref[...] = pack(jnp.concatenate([pieces, blank, theirs], 1))
    extra_own_ref[...] = pack(jnp.concatenate([mine, pieces, blank], 1))


def project(pair, scales, weights, out_weight):
    rows, tokens, channels = pair.shape
    own = weights[0].shape[0]
    return pl.pallas_call(
        project_kernel,
        in_specs=[pl.BlockSpec(memory_space=pl.ANY)] * 10,
        out_specs=[pl.BlockSpec(memory_space=pltpu.VMEM)] * 4,
        out_shape=[
            pltpu.VMEM((own, 2 * rows, tokens), BF16),
            pltpu.VMEM((rows, channels, tokens), BF16),
            pltpu.VMEM((16, 512), BF16),
            pltpu.VMEM((16, 512), BF16),
        ],
        scratch_shapes=[
            pltpu.VMEM((rows, tokens, channels), BF16),
            pltpu.VMEM((16, channels), F32),
            pltpu.VMEM((16, own), F32),
            pltpu.VMEM((4 * own, channels), BF16),
            pltpu.VMEM((own, channels), BF16),
            pltpu.SemaphoreType.DMA,
            pltpu.SemaphoreType.DMA((9,)),
        ],
        name="project",
    )(
        *[
            pltpu.with_memory_space_constraint(a, pltpu.HBM)
            for a in [pair] + [v[None] for v in scales] + weights + [out_weight]
        ]
    )


def scales_of(pieces):
    gain = pieces[:, 0:1] + pieces[:, 1:2] + pieces[:, 2:3]
    return gain, pieces[:, 3:4] + pieces[:, 4:5] + pieces[:, 5:6]


def finish_kernel(mine_ref, other_ref, gate_ref, out_ref, done, sems):
    rows, own, _ = gate_ref.shape
    size = rows * own
    columns, columns_other = unpack(mine_ref[size:]), unpack(other_ref[size:])
    lane = lax.broadcasted_iota(jnp.int32, columns.shape, 1)
    weight = jnp.where(lane < own, columns.astype(F32), columns_other.astype(F32)).astype(BF16)
    gain, bias = scales_of(columns[:, own : own + 8].astype(F32))
    gain_other, bias_other = scales_of(columns_other[:, 0:8].astype(F32))
    copies = [pltpu.make_async_copy(done.at[i], out_ref.at[i], sems.at[i]) for i in range(rows)]
    for i in range(rows):
        mine = mine_ref[i * own : (i + 1) * own].astype(F32)
        other = other_ref[i * own : (i + 1) * own].astype(F32)
        mean = (jnp.sum(mine, 0, keepdims=True) + jnp.sum(other, 0, keepdims=True)) / (2 * own)
        mine, other = mine - mean, other - mean
        square = jnp.sum(mine * mine + other * other, 0, keepdims=True)
        root = lax.rsqrt(square / (2 * own) + EPS)
        onormed = [mine * root * gain + bias, other * root * gain_other + bias_other]
        onormed = jnp.concatenate(onormed, 0).astype(BF16)
        projected = jnp.dot(weight, onormed, preferred_element_type=F32)
        done[i] = (gate_ref[i] * projected).astype(BF16)
        copies[i].start()
    for copy in copies:
        copy.wait()


def finish(mine, other, gate_value):
    rows, own, tokens = gate_value.shape
    operands = [pltpu.with_memory_space_constraint(a, pltpu.VMEM) for a in (mine, other, gate_value)]
    return pl.pallas_call(
        finish_kernel,
        in_specs=[pl.BlockSpec(memory_space=pltpu.VMEM)] * 3,
        out_specs=pl.BlockSpec(memory_space=pl.ANY),
        out_shape=jax.ShapeDtypeStruct((rows, own, tokens), BF16),
        scratch_shapes=[pltpu.VMEM((rows, own, tokens), BF16), pltpu.SemaphoreType.DMA((rows,))],
        name="finish",
    )(*operands)


def body(
    pair,
    norm_gain,
    norm_bias,
    left_weight,
    left_gate,
    right_weight,
    right_gate,
    tri_gain,
    tri_bias,
    out_weight,
    out_gate,
):
    rows, tokens, channels = pair.shape
    own = left_weight.shape[1]

    sent, normed, extra, extra_own = project(
        pair,
        [norm_gain, norm_bias, tri_gain, tri_bias],
        [left_gate.T, left_weight.T, right_gate.T, right_weight.T],
        out_weight,
    )
    first = lax.axis_index("core") == 0
    sent, first = lax.optimization_barrier((sent, first))

    got = lax.all_to_all(sent, CHIPS, 0, 0, tiled=True)
    right_own, got = lax.optimization_barrier((got[:, :rows], got))
    right_other = lax.ppermute(right_own, "core", SWAP)
    own_twice = jnp.concatenate([right_own, right_own], 1)
    right_other, own_twice = lax.optimization_barrier((right_other, own_twice))
    from_own = (lax.broadcasted_iota(jnp.int32, (1, 2 * rows, 1), 1) < rows) == first
    right_all = jnp.where(from_own, own_twice, jnp.concatenate([right_other, right_other], 1))
    triangle = lax.dot_general(
        got[:, rows:].reshape(-1, tokens),
        right_all.reshape(-1, tokens),
        (((1,), (1,)), ((), ())),
        preferred_element_type=F32,
    ).astype(BF16)

    tri = lax.all_to_all(triangle.reshape(own, rows, tokens), CHIPS, 0, 0, tiled=True)
    tri = tri.transpose(1, 0, 2).reshape(-1, tokens)
    other = lax.ppermute(jnp.concatenate([tri, extra], 0), "yhi", SWAP)
    gate_value = jax.nn.sigmoid(per_row(out_gate.T, normed))
    updated = finish(jnp.concatenate([tri, extra_own], 0), other, gate_value)
    return updated.transpose(0, 2, 1)


def solution(mesh):
    fine = Mesh(mesh.devices.reshape(4, 8, 2, 2, 2), RES + ("yhi",))
    placed = (
        P(RES, None, None),
        P(),
        P(),
        P(None, "yhi"),
        P(None, "yhi"),
        P(None, "yhi"),
        P(None, "yhi"),
        P("yhi"),
        P("yhi"),
        P("yhi", None),
        P(None, "yhi"),
    )
    return jax.shard_map(
        body, mesh=fine, in_specs=placed, out_specs=P(RES, None, "yhi"), check_vma=False
    )
```

```python
import jax
import jax.numpy as jnp
from jax import lax
from jax.experimental import pallas as pl
from jax.experimental.pallas import tpu as pltpu
from jax.sharding import Mesh, PartitionSpec as P

F32 = jnp.float32
BF16 = jnp.bfloat16
CHIPS = ("x", "z", "ylo")
RES = CHIPS + ("core",)
EPS = 1e-05
SWAP = [(0, 1), (1, 0)]


def split3(values):
    high = values.astype(BF16)
    rest = values - high.astype(F32)
    middle = rest.astype(BF16)
    return [high, middle, (rest - middle.astype(F32)).astype(BF16)]


def per_row(matrix, values):
    matrix = jnp.broadcast_to(matrix, values.shape[:1] + matrix.shape)
    return lax.dot_general(matrix, values, (((2,), (1,)), ((0,), (0,))), preferred_element_type=F32)


def sigmoid(values):
    return 0.5 * jnp.tanh(0.5 * values) + 0.5


def pack(columns):
    return jnp.concatenate([columns[16 * t : 16 * t + 16] for t in range(4)], 1).astype(BF16)


def unpack(block):
    return jnp.concatenate([block[:, 128 * t : 128 * t + 128] for t in range(4)], 0)


def project_kernel(*refs):
    pair_ref, scale_refs, weight_refs, out_weight_ref = refs[0], refs[1:5], refs[5:9], refs[9]
    sent_ref, normed_ref, out_weight_buf, tri_buf = refs[10:14]
    pair_buf, scale_buf, weight_buf, sem, sems = refs[14:]
    rows, tokens, channels = pair_buf.shape
    own = weight_refs[0].shape[0]
    load = pltpu.make_async_copy(pair_ref, pair_buf, sem)
    load.start()
    copies = [pltpu.make_async_copy(out_weight_ref, out_weight_buf, sems.at[8])]
    for n in range(4):
        place = (scale_buf, tri_buf)[n // 2].at[pl.ds(8 * (n % 2), 1)]
        copies.append(pltpu.make_async_copy(scale_refs[n], place, sems.at[n]))
        place = weight_buf.at[pl.ds(own * n, own)]
        copies.append(pltpu.make_async_copy(weight_refs[n], place, sems.at[4 + n]))
    for copy in copies:
        copy.start()
    row = lax.broadcasted_iota(jnp.int32, (channels, channels), 0)
    column = lax.broadcasted_iota(jnp.int32, (channels, channels), 1)
    centre = (jnp.where(row == column, 1.0, 0.0) - 1 / channels).astype(BF16)
    for copy in copies + [load]:
        copy.wait()

    scales = scale_buf[...].T
    centred = lax.dot_general(
        centre,
        pair_buf[...].reshape(rows * tokens, channels),
        (((1,), (1,)), ((), ())),
        preferred_element_type=F32,
    )
    var = jnp.mean(centred * centred, 0, keepdims=True)
    normed = centred * lax.rsqrt(var + EPS) * scales[:, 0:1] + scales[:, 8:9]
    normed = normed.astype(BF16)
    pre = jnp.dot(weight_buf[...], normed, preferred_element_type=F32)
    left, right = [], []
    for i in range(rows):
        at = slice(i * tokens, (i + 1) * tokens)
        normed_ref[i] = normed[:, at]
        left.append((sigmoid(pre[:own, at]) * pre[own : 2 * own, at]).astype(BF16))
        right.append((sigmoid(pre[2 * own : 3 * own, at]) * pre[3 * own :, at]).astype(BF16))
    sent_ref[...] = jnp.swapaxes(jnp.stack(right + left, 0), 0, 1)


def pack_kernel(out_weight_ref, tri_ref, extra_ref, extra_own_ref):
    own, channels = out_weight_ref.shape
    pieces = [piece.astype(F32) for n in (0, 8) for piece in split3(tri_ref[n : n + 1])]
    pieces = jnp.concatenate(pieces + [jnp.zeros_like(pieces[0])] * 2, 0).T
    blank = jnp.zeros((own, channels - own - 8), F32)
    columns = out_weight_ref[...].astype(F32).T
    low = lax.axis_index("yhi") == 0
    mine = jnp.where(low, columns[:own], columns[own:])
    theirs = jnp.where(low, columns[own:], columns[:own])
    extra_ref[...] = pack(jnp.concatenate([pieces, blank, theirs], 1))
    extra_own_ref[...] = pack(jnp.concatenate([mine, pieces, blank], 1))


def pack_extra(out_weight, scales):
    operands = [pltpu.with_memory_space_constraint(a, pltpu.VMEM) for a in (out_weight, scales)]
    return pl.pallas_call(
        pack_kernel,
        in_specs=[pl.BlockSpec(memory_space=pltpu.VMEM)] * 2,
        out_specs=[pl.BlockSpec(memory_space=pltpu.VMEM)] * 2,
        out_shape=[pltpu.VMEM((16, 512), BF16)] * 2,
        name="pack",
    )(*operands)


def project(pair, scales, weights, out_weight):
    rows, tokens, channels = pair.shape
    own = weights[0].shape[0]
    return pl.pallas_call(
        project_kernel,
        in_specs=[pl.BlockSpec(memory_space=pl.ANY)] * 10,
        out_specs=[pl.BlockSpec(memory_space=pltpu.VMEM)] * 4,
        out_shape=[
            pltpu.VMEM((own, 2 * rows, tokens), BF16),
            pltpu.VMEM((rows, channels, tokens), BF16),
            pltpu.VMEM((own, channels), BF16),
            pltpu.VMEM((16, own), F32),
        ],
        scratch_shapes=[
            pltpu.VMEM((rows, tokens, channels), BF16),
            pltpu.VMEM((16, channels), F32),
            pltpu.VMEM((4 * own, channels), BF16),
            pltpu.SemaphoreType.DMA,
            pltpu.SemaphoreType.DMA((9,)),
        ],
        name="project",
    )(
        *[
            pltpu.with_memory_space_constraint(a, pltpu.HBM)
            for a in [pair] + [v[None] for v in scales] + weights + [out_weight]
        ]
    )


def scales_of(pieces):
    gain = pieces[:, 0:1] + pieces[:, 1:2] + pieces[:, 2:3]
    return gain, pieces[:, 3:4] + pieces[:, 4:5] + pieces[:, 5:6]


def finish_kernel(mine_ref, other_ref, gate_ref, out_ref, done, sems):
    rows, own, _ = gate_ref.shape
    size = rows * own
    columns, columns_other = unpack(mine_ref[size:]), unpack(other_ref[size:])
    lane = lax.broadcasted_iota(jnp.int32, columns.shape, 1)
    weight = jnp.where(lane < own, columns.astype(F32), columns_other.astype(F32)).astype(BF16)
    gain, bias = scales_of(columns[:, own : own + 8].astype(F32))
    gain_other, bias_other = scales_of(columns_other[:, 0:8].astype(F32))
    copies = [pltpu.make_async_copy(done.at[i], out_ref.at[i], sems.at[i]) for i in range(rows)]
    for i in range(rows):
        mine = mine_ref[i * own : (i + 1) * own].astype(F32)
        other = other_ref[i * own : (i + 1) * own].astype(F32)
        mean = (jnp.sum(mine, 0, keepdims=True) + jnp.sum(other, 0, keepdims=True)) / (2 * own)
        mine, other = mine - mean, other - mean
        square = jnp.sum(mine * mine + other * other, 0, keepdims=True)
        root = lax.rsqrt(square / (2 * own) + EPS)
        onormed = [mine * root * gain + bias, other * root * gain_other + bias_other]
        onormed = jnp.concatenate(onormed, 0).astype(BF16)
        projected = jnp.dot(weight, onormed, preferred_element_type=F32)
        done[i] = (gate_ref[i] * projected).astype(BF16)
        copies[i].start()
    for copy in copies:
        copy.wait()


def finish(mine, other, gate_value):
    rows, own, tokens = gate_value.shape
    operands = [pltpu.with_memory_space_constraint(a, pltpu.VMEM) for a in (mine, other, gate_value)]
    return pl.pallas_call(
        finish_kernel,
        in_specs=[pl.BlockSpec(memory_space=pltpu.VMEM)] * 3,
        out_specs=pl.BlockSpec(memory_space=pl.ANY),
        out_shape=jax.ShapeDtypeStruct((rows, own, tokens), BF16),
        scratch_shapes=[pltpu.VMEM((rows, own, tokens), BF16), pltpu.SemaphoreType.DMA((rows,))],
        name="finish",
    )(*operands)


def body(
    pair,
    norm_gain,
    norm_bias,
    left_weight,
    left_gate,
    right_weight,
    right_gate,
    tri_gain,
    tri_bias,
    out_weight,
    out_gate,
):
    rows, tokens, channels = pair.shape
    own = left_weight.shape[1]

    sent, normed, out_raw, tri_raw = project(
        pair,
        [norm_gain, norm_bias, tri_gain, tri_bias],
        [left_gate.T, left_weight.T, right_gate.T, right_weight.T],
        out_weight,
    )
    first = lax.axis_index("core") == 0
    sent, first = lax.optimization_barrier((sent, first))

    got = lax.all_to_all(sent, CHIPS, 0, 0, tiled=True)
    right_own, got, out_raw, tri_raw = lax.optimization_barrier(
        (got[:, :rows], got, out_raw, tri_raw)
    )
    right_other = lax.ppermute(right_own, "core", SWAP)
    own_twice = jnp.concatenate([right_own, right_own], 1)
    extra, extra_own = pack_extra(out_raw, tri_raw)
    right_other, own_twice, extra, extra_own = lax.optimization_barrier(
        (right_other, own_twice, extra, extra_own)
    )
    from_own = (lax.broadcasted_iota(jnp.int32, (1, 2 * rows, 1), 1) < rows) == first
    right_all = jnp.where(from_own, own_twice, jnp.concatenate([right_other, right_other], 1))
    triangle = lax.dot_general(
        got[:, rows:].reshape(-1, tokens),
        right_all.reshape(-1, tokens),
        (((1,), (1,)), ((), ())),
        preferred_element_type=F32,
    ).astype(BF16)

    tri = lax.all_to_all(triangle.reshape(own, rows, tokens), CHIPS, 0, 0, tiled=True)
    tri = tri.transpose(1, 0, 2).reshape(-1, tokens)
    other = lax.ppermute(jnp.concatenate([tri, extra], 0), "yhi", SWAP)
    gate_value = jax.nn.sigmoid(per_row(out_gate.T, normed))
    updated = finish(jnp.concatenate([tri, extra_own], 0), other, gate_value)
    return updated.transpose(0, 2, 1)


def solution(mesh):
    fine = Mesh(mesh.devices.reshape(4, 8, 2, 2, 2), RES + ("yhi",))
    placed = (
        P(RES, None, None),
        P(),
        P(),
        P(None, "yhi"),
        P(None, "yhi"),
        P(None, "yhi"),
        P(None, "yhi"),
        P("yhi"),
        P("yhi"),
        P("yhi", None),
        P(None, "yhi"),
    )
    return jax.shard_map(
        body, mesh=fine, in_specs=placed, out_specs=P(RES, None, "yhi"), check_vma=False
    )
```

```python
import jax
import jax.numpy as jnp
from jax import lax
from jax.experimental import pallas as pl
from jax.experimental.pallas import tpu as pltpu
from jax.sharding import Mesh, PartitionSpec as P

F32 = jnp.float32
BF16 = jnp.bfloat16
CHIPS = ("x", "z", "ylo")
RES = CHIPS + ("core",)
EPS = 1e-05
SWAP = [(0, 1), (1, 0)]


def split3(values):
    high = values.astype(BF16)
    rest = values - high.astype(F32)
    middle = rest.astype(BF16)
    return [high, middle, (rest - middle.astype(F32)).astype(BF16)]


def per_row(matrix, values):
    matrix = jnp.broadcast_to(matrix, values.shape[:1] + matrix.shape)
    return lax.dot_general(matrix, values, (((2,), (1,)), ((0,), (0,))), preferred_element_type=F32)


def sigmoid(values):
    return 0.5 * jnp.tanh(0.5 * values) + 0.5


def pack(columns):
    return jnp.concatenate([columns[16 * t : 16 * t + 16] for t in range(4)], 1).astype(BF16)


def unpack(block):
    return jnp.concatenate([block[:, 128 * t : 128 * t + 128] for t in range(4)], 0)


def project_kernel(*refs):
    pair_ref, scale_refs, weight_refs, out_weight_ref = refs[0], refs[1:5], refs[5:9], refs[9]
    sent_ref, normed_ref, out_weight_buf, tri_buf = refs[10:14]
    pair_buf, scale_buf, weight_buf, sem, sems = refs[14:]
    rows, tokens, channels = pair_buf.shape
    own = weight_refs[0].shape[0]
    load = pltpu.make_async_copy(pair_ref, pair_buf, sem)
    load.start()
    copies = [pltpu.make_async_copy(out_weight_ref, out_weight_buf, sems.at[8])]
    for n in range(4):
        place = (scale_buf, tri_buf)[n // 2].at[pl.ds(8 * (n % 2), 1)]
        copies.append(pltpu.make_async_copy(scale_refs[n], place, sems.at[n]))
        place = weight_buf.at[pl.ds(own * n, own)]
        copies.append(pltpu.make_async_copy(weight_refs[n], place, sems.at[4 + n]))
    for copy in copies:
        copy.start()
    row = lax.broadcasted_iota(jnp.int32, (channels, channels), 0)
    column = lax.broadcasted_iota(jnp.int32, (channels, channels), 1)
    centre = (jnp.where(row == column, 1.0, 0.0) - 1 / channels).astype(BF16)
    for copy in copies + [load]:
        copy.wait()

    scales = scale_buf[...].T
    centred = lax.dot_general(
        centre,
        pair_buf[...].reshape(rows * tokens, channels),
        (((1,), (1,)), ((), ())),
        preferred_element_type=F32,
    )
    var = jnp.mean(centred * centred, 0, keepdims=True)
    normed = centred * lax.rsqrt(var + EPS) * scales[:, 0:1] + scales[:, 8:9]
    normed = normed.astype(BF16)
    pre = jnp.dot(weight_buf[...], normed, preferred_element_type=F32)
    left, right = [], []
    for i in range(rows):
        at = slice(i * tokens, (i + 1) * tokens)
        normed_ref[i] = normed[:, at]
        left.append((sigmoid(pre[:own, at]) * pre[own : 2 * own, at]).astype(BF16))
        right.append((sigmoid(pre[2 * own : 3 * own, at]) * pre[3 * own :, at]).astype(BF16))
    sent_ref[...] = jnp.swapaxes(jnp.stack(right + left, 0), 0, 1)


def pack_kernel(out_weight_ref, tri_ref, extra_ref, extra_own_ref):
    own, channels = out_weight_ref.shape
    pieces = [piece.astype(F32) for n in (0, 8) for piece in split3(tri_ref[n : n + 1])]
    pieces = jnp.concatenate(pieces + [jnp.zeros_like(pieces[0])] * 2, 0).T
    blank = jnp.zeros((own, channels - own - 8), F32)
    columns = out_weight_ref[...].astype(F32).T
    low = lax.axis_index("yhi") == 0
    mine = jnp.where(low, columns[:own], columns[own:])
    theirs = jnp.where(low, columns[own:], columns[:own])
    extra_ref[...] = pack(jnp.concatenate([pieces, blank, theirs], 1))
    extra_own_ref[...] = pack(jnp.concatenate([mine, pieces, blank], 1))


def pack_extra(out_weight, scales):
    operands = [pltpu.with_memory_space_constraint(a, pltpu.VMEM) for a in (out_weight, scales)]
    return pl.pallas_call(
        pack_kernel,
        in_specs=[pl.BlockSpec(memory_space=pltpu.VMEM)] * 2,
        out_specs=[pl.BlockSpec(memory_space=pltpu.VMEM)] * 2,
        out_shape=[pltpu.VMEM((16, 512), BF16)] * 2,
        name="pack",
    )(*operands)


def project(pair, scales, weights, out_weight):
    rows, tokens, channels = pair.shape
    own = weights[0].shape[0]
    return pl.pallas_call(
        project_kernel,
        in_specs=[pl.BlockSpec(memory_space=pl.ANY)] * 10,
        out_specs=[pl.BlockSpec(memory_space=pltpu.VMEM)] * 4,
        out_shape=[
            pltpu.VMEM((own, 2 * rows, tokens), BF16),
            pltpu.VMEM((rows, channels, tokens), BF16),
            pltpu.VMEM((own, channels), BF16),
            pltpu.VMEM((16, own), F32),
        ],
        scratch_shapes=[
            pltpu.VMEM((rows, tokens, channels), BF16),
            pltpu.VMEM((16, channels), F32),
            pltpu.VMEM((4 * own, channels), BF16),
            pltpu.SemaphoreType.DMA,
            pltpu.SemaphoreType.DMA((9,)),
        ],
        name="project",
    )(
        *[
            pltpu.with_memory_space_constraint(a, pltpu.HBM)
            for a in [pair] + [v[None] for v in scales] + weights + [out_weight]
        ]
    )


def scales_of(pieces):
    gain = pieces[:, 0:1] + pieces[:, 1:2] + pieces[:, 2:3]
    return gain, pieces[:, 3:4] + pieces[:, 4:5] + pieces[:, 5:6]


def finish_kernel(mine_ref, extra_ref, other_ref, gate_ref, out_ref, done, sems):
    rows, own, _ = gate_ref.shape
    size = rows * own
    columns, columns_other = unpack(extra_ref[...]), unpack(other_ref[size:])
    lane = lax.broadcasted_iota(jnp.int32, columns.shape, 1)
    weight = jnp.where(lane < own, columns.astype(F32), columns_other.astype(F32)).astype(BF16)
    gain, bias = scales_of(columns[:, own : own + 8].astype(F32))
    gain_other, bias_other = scales_of(columns_other[:, 0:8].astype(F32))
    copies = [pltpu.make_async_copy(done.at[i], out_ref.at[i], sems.at[i]) for i in range(rows)]
    for i in range(rows):
        mine = mine_ref[i * own : (i + 1) * own].astype(F32)
        other = other_ref[i * own : (i + 1) * own].astype(F32)
        mean = (jnp.sum(mine, 0, keepdims=True) + jnp.sum(other, 0, keepdims=True)) / (2 * own)
        mine, other = mine - mean, other - mean
        square = jnp.sum(mine * mine + other * other, 0, keepdims=True)
        root = lax.rsqrt(square / (2 * own) + EPS)
        onormed = [mine * root * gain + bias, other * root * gain_other + bias_other]
        onormed = jnp.concatenate(onormed, 0).astype(BF16)
        projected = jnp.dot(weight, onormed, preferred_element_type=F32)
        done[i] = (gate_ref[i] * projected).astype(BF16)
        copies[i].start()
    for copy in copies:
        copy.wait()


def finish(*operands):
    rows, own, tokens = operands[-1].shape
    operands = [pltpu.with_memory_space_constraint(a, pltpu.VMEM) for a in operands]
    return pl.pallas_call(
        finish_kernel,
        in_specs=[pl.BlockSpec(memory_space=pltpu.VMEM)] * 4,
        out_specs=pl.BlockSpec(memory_space=pl.ANY),
        out_shape=jax.ShapeDtypeStruct((rows, own, tokens), BF16),
        scratch_shapes=[pltpu.VMEM((rows, own, tokens), BF16), pltpu.SemaphoreType.DMA((rows,))],
        name="finish",
    )(*operands)


def body(
    pair,
    norm_gain,
    norm_bias,
    left_weight,
    left_gate,
    right_weight,
    right_gate,
    tri_gain,
    tri_bias,
    out_weight,
    out_gate,
):
    rows, tokens, channels = pair.shape
    own = left_weight.shape[1]

    sent, normed, out_raw, tri_raw = project(
        pair,
        [norm_gain, norm_bias, tri_gain, tri_bias],
        [left_gate.T, left_weight.T, right_gate.T, right_weight.T],
        out_weight,
    )
    first = lax.axis_index("core") == 0
    sent, first = lax.optimization_barrier((sent, first))

    got = lax.all_to_all(sent, CHIPS, 0, 0, tiled=True)
    right_own, got, out_raw, tri_raw = lax.optimization_barrier(
        (got[:, :rows], got, out_raw, tri_raw)
    )
    right_other = lax.ppermute(right_own, "core", SWAP)
    own_twice = jnp.concatenate([right_own, right_own], 1)
    extra, extra_own = pack_extra(out_raw, tri_raw)
    right_other, own_twice, extra, extra_own = lax.optimization_barrier(
        (right_other, own_twice, extra, extra_own)
    )
    from_own = (lax.broadcasted_iota(jnp.int32, (1, 2 * rows, 1), 1) < rows) == first
    right_all = jnp.where(from_own, own_twice, jnp.concatenate([right_other, right_other], 1))
    triangle = lax.dot_general(
        got[:, rows:].reshape(-1, tokens),
        right_all.reshape(-1, tokens),
        (((1,), (1,)), ((), ())),
        preferred_element_type=F32,
    ).astype(BF16)

    tri = lax.all_to_all(triangle.reshape(own, rows, tokens), CHIPS, 0, 0, tiled=True)
    tri = tri.transpose(1, 0, 2).reshape(-1, tokens)
    mine = jnp.concatenate([tri, extra], 0)
    other = lax.ppermute(mine, "yhi", SWAP)
    gate_value = jax.nn.sigmoid(per_row(out_gate.T, normed))
    updated = finish(mine, extra_own, other, gate_value)
    return updated.transpose(0, 2, 1)


def solution(mesh):
    fine = Mesh(mesh.devices.reshape(4, 8, 2, 2, 2), RES + ("yhi",))
    placed = (
        P(RES, None, None),
        P(),
        P(),
        P(None, "yhi"),
        P(None, "yhi"),
        P(None, "yhi"),
        P(None, "yhi"),
        P("yhi"),
        P("yhi"),
        P("yhi", None),
        P(None, "yhi"),
    )
    return jax.shard_map(
        body, mesh=fine, in_specs=placed, out_specs=P(RES, None, "yhi"), check_vma=False
    )
```
